128 devices in a mesh: zero: 32 (over x, z, core), expert: 4 (over y).
Axes of the slice: x: 4, y: 4, z: 4, core: 2. Of those that a mesh axis runs over, the one named last changes fastest.
Arguments:
- grad: bfloat16 [48, 576, 7168], P('expert', 'zero'), may hold values from -6 to 6
- momentum: float32 [48, 576, 7168], P('expert', 'zero'), may hold values from -6 to 6
- backup: float32 [48, 576, 7168], P('expert', 'zero'), may hold values from -6 to 6
- recovery: int32 [4], replicated, may hold values from 0 to 31
Outputs:
- new_momentum: float32 [48, 576, 7168], P('expert', 'zero')
- update: bfloat16 [48, 576, 7168], P('expert', 'zero')
The draws below stay inside these ranges and needn't reach their ends.
All inputs are finite; a program needn't handle non-finite values.
Results may differ from the reference program's by a relative error of at most 0.006.
Values may be sent and summed in bfloat16 or wider, within the bound.
A program may use at most 192 MiB of HBM per device.

```python
import jax
import jax.numpy as jnp
from jax import lax

MODEL_WIDTH = 7168
ITERS = 3
R = 576
MATS_GRP = 12
MATS = 48
ROWS_DEV = 18
N_ZERO = 32
N_EXPERT = 4


def draw_recovery(key, part):
    key = jax.random.fold_in(key, 11)
    first, second = jax.random.split(key)
    values = jax.random.randint(first, (N_EXPERT,), 0, N_ZERO)
    order = jax.random.permutation(second, N_EXPERT)
    values = values.at[order[0]].set(N_ZERO - 1)
    values = values.at[order[1]].set(0)
    return values.astype(jnp.int32)


def block_scale(rng, extent, pieces, least, largest):
    factor_of = 1.0
    for dim, blocks in pieces:
        heights = jax.random.uniform(jax.random.fold_in(jax.random.fold_in(rng, 6), dim), (blocks,), jnp.float32, least / len(pieces), largest / len(pieces))
        factor_of = factor_of * jnp.repeat(jnp.exp(heights), extent[dim] // blocks).reshape((-1,) + (1,) * (len(extent) - 1 - dim))
    return factor_of


def centred(key, dims, deviation, reach, shards=(), kind=jnp.bfloat16):
    values = jax.random.normal(key, dims, jnp.float32) * deviation
    if len(shards) > 0:
        values = block_scale(key, dims, shards, -0.22, 0.18) * values
    return jnp.clip(values, min=-reach, max=reach).astype(kind)


def setup_inputs(seed: int = 0) -> dict:
    key_of = jax.random.split(jax.random.key(seed), 5)
    grad = centred(key_of[0], (MATS, R, MODEL_WIDTH), 1.0, 6.0, ((0, 4), (1, 32)))
    momentum = centred(key_of[1], (MATS, R, MODEL_WIDTH), 1.0, 6.0, ((0, 4), (1, 32)), jnp.float32)
    backup = centred(key_of[2], (MATS, R, MODEL_WIDTH), 1.0, 6.0, ((0, 4), (1, 32)), jnp.float32)
    recovery = draw_recovery(jax.random.fold_in(key_of[4], 71), 0)
    return {"grad": grad, "momentum": momentum, "backup": backup, "recovery": recovery}


beta = 0.95
coef_a = 3.4445
coef_b = -4.775
coef_c = 2.0315
eps = 1e-07
highest = lax.Precision.HIGHEST

def mult(left, right):
    return jnp.dot(left, right, precision=highest, preferred_element_type=jnp.float32)

def newton_orthonormal(matrix):
    norm = jnp.sqrt(jnp.sum(matrix * matrix))
    start = matrix / (norm + eps)
    gram = mult(start, start.T)
    order = gram.shape[0]
    identity = jnp.eye(order, dtype=jnp.float32)
    product = identity
    for step in range(ITERS):
        poly = coef_a * identity + coef_b * gram + coef_c * mult(gram, gram)
        gram = mult(poly, mult(gram, poly))
        product = mult(poly, product)
    return mult(product, start)

def reference(grad, momentum, backup, recovery):
    live = momentum
    nought = jnp.int32(0)
    for group in range(N_EXPERT):
        mirror_group = (group + N_EXPERT - 1) % N_EXPERT
        start_rows = (recovery[group].astype(jnp.int32) * ROWS_DEV).astype(jnp.int32)
        copied = lax.dynamic_slice(backup, (jnp.int32(mirror_group * MATS_GRP), start_rows, nought), (MATS_GRP, ROWS_DEV, MODEL_WIDTH))
        live = lax.dynamic_update_slice(live, copied, (jnp.int32(group * MATS_GRP), start_rows, nought))
    gradient_wide = grad.astype(jnp.float32)
    new_momentum = beta * live + gradient_wide
    blend = gradient_wide + beta * new_momentum
    ortho = lax.map(newton_orthonormal, blend)
    scale_factor = 0.2 * max(R, MODEL_WIDTH) ** 0.5
    update = (ortho * scale_factor).astype(jnp.bfloat16)
    return (new_momentum, update)
```

```python
import jax
import jax.numpy as jnp
from jax import lax
from jax.experimental import pallas as pl
from jax.experimental.pallas import tpu as pltpu
from jax.sharding import PartitionSpec as P

MODEL_WIDTH = 7168
R = 576
MATS_GRP = 12
ROWS_DEV = 18
N_ZERO = 32
N_EXPERT = 4

beta = 0.95
coef_a = 3.4445
coef_b = -4.775
coef_c = 2.0315
eps = 1e-07
SCALE = 0.2 * max(R, MODEL_WIDTH) ** 0.5

CHUNKS = 8
CHUNK = MODEL_WIDTH // CHUNKS
PIECES = CHUNK // 128
UNIT = CHUNK + 128
MAIN = 16 * N_ZERO
HALF = R // 2

OWNER_CHIP = (0, 2, 5, 3, 11, 6, 4, 12, 9, 13, 15, 10)
HUB_CHIP = (1, 7, 8, 14)
TEAM_OF = (0, 0, 0, 1, 2, 0, 1, 1, 2, 2, 3, 1, 2, 3, 3, 3)
SPOT_OF = (0, 3, 1, 0, 0, 2, 2, 3, 3, 2, 2, 1, 1, 0, 3, 1)

STEPS = ((0, 0), (1, 0), (0, 1), (3, 0), (0, 3), (2, 0), (0, 2), (1, 1),
         (3, 3), (1, 3), (3, 1), (2, 1), (1, 2), (2, 3), (3, 2), (2, 2))

MESH = pl.DeviceIdType.MESH
f32 = jnp.float32
bf16 = jnp.bfloat16


def lut(index, table):
    value = jnp.int32(table[0])
    for place, entry in enumerate(table):
        if place:
            value = jnp.where(index == place, jnp.int32(entry), value)
    return value


def pack_rest(rest):
    pieces = [rest[:, 128 * g : 128 * (g + 1)] for g in range(PIECES)]
    return jnp.concatenate(pieces + [jnp.zeros((2, 128), rest.dtype)], axis=0)


def unpack_rest(tile):
    return jnp.concatenate([tile[2 * g : 2 * g + 2] for g in range(PIECES)], axis=1)


def times(left, right):
    return jnp.dot(left, right, preferred_element_type=f32)


def main_kernel(
    flags, grad, mom, back, out_ref, live_ref,
    gv, mv, bv, own, other, joined, shifted, units, x, o, perm, gram, gsend, gpeer, ghalf, gin, q,
    ma, mb, mc, md,
    in_sem, d_send, d_recv, y_send, y_recv, f_send, f_recv, a_send, a_recv, v_sem,
    g_send, g_recv, h_send, h_recv, k_send, k_recv, q_send, q_recv, p_send, p_recv, o_send, o_recv,
):
    zero, expert = lax.axis_index("zero"), lax.axis_index("expert")
    core = lax.rem(zero, 2)
    chip = zero // 2
    cx, cz = chip // 4, lax.rem(chip, 4)
    team, spot = lut(chip, TEAM_OF), lut(chip, SPOT_OF)
    is_owner = spot < 3
    is_hub = spot == 3
    twin = zero + 1 - 2 * core
    up = lax.rem(expert + 1, N_EXPERT)
    down = lax.rem(expert + N_EXPERT - 1, N_EXPERT)
    mine = pl.ds(4 * core, 4)
    theirs = pl.ds(4 - 4 * core, 4)
    lost = flags[0]
    mirror = flags[1]

    barrier = pltpu.get_barrier_semaphore()

    def greet(i, carry):
        pl.semaphore_signal(
            barrier, inc=1, device_id=(lax.rem(zero + i, N_ZERO), expert), device_id_type=MESH)
        return carry

    lax.fori_loop(1, N_ZERO, greet, 0)
    pl.semaphore_signal(barrier, inc=1, device_id=(zero, up), device_id_type=MESH)
    pl.semaphore_signal(barrier, inc=1, device_id=(zero, down), device_id_type=MESH)

    def matrix_at(i):
        return lax.rem(i + chip, MATS_GRP)

    def load(i, carry):
        m = matrix_at(i)
        pltpu.make_async_copy(back.at[m], bv.at[m], in_sem.at[0, m]).start()
        pltpu.make_async_copy(grad.at[m], gv.at[m], in_sem.at[1, m]).start()
        pltpu.make_async_copy(mom.at[m], mv.at[m], in_sem.at[2, m]).start()
        return carry

    lax.fori_loop(0, MATS_GRP, load, 0)

    rows = lax.broadcasted_iota(jnp.int32, (MAIN, MAIN), 0)
    cols = lax.broadcasted_iota(jnp.int32, (MAIN, MAIN), 1)
    wanted = 16 * (lax.rem(rows, 64) // 2) + 2 * (rows // 64) + lax.rem(rows, 2)
    perm[...] = jnp.where(cols == wanted, 1.0, 0.0).astype(bf16)

    pl.semaphore_wait(barrier, N_ZERO + 1)

    def to_twin(m):
        return pltpu.make_async_remote_copy(
            own.at[m, theirs], other.at[m], d_send.at[m], d_recv.at[m],
            device_id=(twin, expert), device_id_type=MESH)

    def to_up(m):
        return pltpu.make_async_remote_copy(
            joined.at[m], shifted.at[m, mine], y_send.at[m], y_recv.at[m],
            device_id=(zero, up), device_id_type=MESH)

    def forward(m):
        return pltpu.make_async_remote_copy(
            shifted.at[m, mine], shifted.at[m, mine], f_send.at[m], f_recv.at[m],
            device_id=(twin, expert), device_id_type=MESH)

    def forwarded(m):
        return pltpu.make_async_remote_copy(
            shifted.at[m, theirs], shifted.at[m, theirs], f_send.at[m], f_recv.at[m],
            device_id=(twin, expert), device_id_type=MESH)

    def keep(m):
        return pltpu.make_async_copy(shifted.at[m], live_ref.at[m], v_sem.at[m])

    def deliver(source, place, target):
        @pl.when(target != zero)
        def _():
            pltpu.make_async_remote_copy(
                source, place, a_send, a_recv, device_id=(target, expert), device_id_type=MESH).start()

        @pl.when(target == zero)
        def _():
            pltpu.make_async_copy(source, place, a_recv).start()

    my_rows = pl.ds(16 * zero, 16)

    def stage(i, carry):
        @pl.when(i < MATS_GRP)
        def _():
            m = matrix_at(i)
            pltpu.make_async_copy(back.at[m], bv.at[m], in_sem.at[0, m]).wait()
            for k in range(CHUNKS):
                span = pl.ds(CHUNK * k, CHUNK)
                own[m, k, :, :CHUNK] = (bv[m, :16, span] * mirror).astype(bf16)
                own[m, k, :, CHUNK:] = pack_rest(bv[m, 16:, span] * mirror).astype(bf16)
            to_twin(m).start()

        @pl.when(jnp.logical_and(i >= 1, i < MATS_GRP + 1))
        def _():
            m = matrix_at(i - 1)
            to_twin(m).wait_recv()
            joined[m] = own[m, mine] + other[m]
            to_up(m).start()

        @pl.when(jnp.logical_and(i >= 2, i < MATS_GRP + 2))
        def _():
            m = matrix_at(i - 2)
            to_up(m).wait_recv()
            forward(m).start()

        @pl.when(i >= 3)
        def _():
            m = matrix_at(i - 3)
            forwarded(m).wait_recv()
            keep(m).start()
            pltpu.make_async_copy(grad.at[m], gv.at[m], in_sem.at[1, m]).wait()
            pltpu.make_async_copy(mom.at[m], mv.at[m], in_sem.at[2, m]).wait()
            stale = (beta * beta) * (1.0 - lost)
            fresh = (beta * beta) * lost
            for k in range(CHUNKS):
                span = pl.ds(CHUNK * k, CHUNK)
                top = (1.0 + beta) * gv[m, :16, span].astype(f32) + stale * mv[m, :16, span]
                units[m, k, :, :CHUNK] = (
                    top + fresh * shifted[m, k, :, :CHUNK].astype(f32)).astype(bf16)
                rest = (1.0 + beta) * gv[m, 16:, span].astype(f32) + stale * mv[m, 16:, span]
                units[m, k, :, CHUNK:] = (
                    pack_rest(rest) + fresh * shifted[m, k, :, CHUNK:].astype(f32)).astype(bf16)
            hub, j, owner = lut(m // 3, HUB_CHIP), lax.rem(m, 3), lut(m, OWNER_CHIP)
            for c in range(2):
                deliver(units.at[m, pl.ds(6 + c, 1)], x.at[pl.ds(j, 1), my_rows], 2 * hub + c)
            for c in range(2):
                deliver(units.at[m, pl.ds(3 * c, 3)], x.at[:, my_rows], 2 * owner + c)
        return carry

    lax.fori_loop(0, MATS_GRP + 3, stage, 0)

    pltpu.make_async_copy(x.at[:, pl.ds(0, MAIN)], x.at[:, pl.ds(0, MAIN)], a_recv).wait()

    packed = jnp.concatenate([x[s, :MAIN, CHUNK:] for s in range(3)], axis=1)
    rest = times(perm[...], packed).astype(bf16)
    for s in range(3):
        for g in range(PIECES):
            x[s, MAIN:, 128 * g : 128 * (g + 1)] = rest[64 * g : 64 * (g + 1), 128 * s : 128 * (s + 1)]

    for s in range(3):
        block = x[s, :, :CHUNK]
        gram[s] = lax.dot_general(block, block, (((1,), (1,)), ((), ())), preferred_element_type=f32)

    my_half = pl.ds(HALF * core, HALF)
    their_half = pl.ds(HALF - HALF * core, HALF)

    def hub_to_twin():
        return pltpu.make_async_remote_copy(
            gsend.at[:, their_half], ghalf, h_send, h_recv,
            device_id=(twin, expert), device_id_type=MESH)

    def hub_to_owner(s):
        return pltpu.make_async_remote_copy(
            ghalf.at[s], gin.at[my_half], k_send.at[s], k_recv,
            device_id=(2 * lut(3 * team + s, OWNER_CHIP) + core, expert), device_id_type=MESH)

    def gram_to_twin():
        return pltpu.make_async_remote_copy(
            gram.at[0], gpeer, g_send, g_recv, device_id=(twin, expert), device_id_type=MESH)

    def half_to_twin():
        return pltpu.make_async_remote_copy(
            gin.at[my_half], gin.at[my_half], q_send.at[0], q_recv.at[0],
            device_id=(twin, expert), device_id_type=MESH)

    def poly_to_hub():
        return pltpu.make_async_remote_copy(
            q.at[0, my_half], q.at[spot, my_half], p_send.at[0], p_recv.at[spot],
            device_id=(2 * lut(team, HUB_CHIP) + core, expert), device_id_type=MESH)

    def poly_here(s):
        return pltpu.make_async_copy(q.at[s, my_half], q.at[s, my_half], p_recv.at[s])

    def poly_to_twin(s):
        return pltpu.make_async_remote_copy(
            q.at[s, my_half], q.at[s, my_half], q_send.at[s], q_recv.at[s],
            device_id=(twin, expert), device_id_type=MESH)

    @pl.when(is_hub)
    def _():
        for s in range(3):
            gsend[s] = gram[s].astype(bf16)
        hub_to_twin().start()
        hub_to_twin().wait_recv()
        for s in range(3):
            ghalf[s] = (gram[s, my_half] + ghalf[s].astype(f32)).astype(bf16)
            hub_to_owner(s).start()
        hub_to_twin().wait_send()
        for s in range(3):
            poly_here(s).wait()
            poly_to_twin(s).start()
        for s in range(3):
            hub_to_owner(s).wait_send()
            poly_to_twin(s).wait()

    @pl.when(is_owner)
    def _():
        gram[0] = gram[0] + gram[1] + gram[2]
        gram_to_twin().start()
        pltpu.make_async_copy(gin.at[my_half], gin.at[my_half], k_recv).wait()
        half_to_twin().start()
        gram_to_twin().wait()
        total = gram[0] + gpeer[...]
        half_to_twin().wait()
        total = total + gin[...].astype(f32)
        eye = (lax.broadcasted_iota(jnp.int32, (R, R), 0)
               == lax.broadcasted_iota(jnp.int32, (R, R), 1))
        norm = jnp.sqrt(jnp.sum(jnp.where(eye, total, 0.0)))
        inverse = 1.0 / (norm + eps)
        a, b, c = coef_a, coef_b, coef_c
        ga = total * (inverse * inverse)
        ma[...] = ga.astype(bf16)
        gram[0] = ga
        d1 = b * gram[0] + c * times(ma[...], ma[...])
        gram[1] = d1
        mb[...] = d1.astype(bf16)
        mc[...] = (2.0 * a * gram[1] + times(mb[...], mb[...])).astype(bf16)
        a1 = a * a * gram[0] + times(ma[...], mc[...])
        gram[0] = a1
        ma[...] = a1.astype(bf16)
        d2 = b * gram[0] + c * times(ma[...], ma[...])
        gram[2] = d2
        mc[...] = d2.astype(bf16)
        gram[1] = a * (gram[1] + gram[2]) + times(mb[...], mc[...])
        md[...] = (2.0 * a * gram[2] + times(mc[...], mc[...])).astype(bf16)
        a2 = a * a * gram[0] + times(ma[...], md[...])
        gram[0] = a2
        ma[...] = a2.astype(bf16)
        d3 = b * gram[0] + c * times(ma[...], ma[...])
        gram[2] = d3
        mb[...] = d3.astype(bf16)
        mc[...] = gram[1].astype(bf16)
        poly = a * gram[1] + a * a * gram[2] + times(mc[...], mb[...])
        poly = jnp.where(eye, poly + a * a * a, poly)
        q[0] = (poly * (inverse * SCALE)).astype(bf16)
        poly_to_hub().start()

    def outgoing(s, target):
        m = 3 * team + jnp.where(is_owner, spot, s)
        k = jnp.where(is_owner, 3 * core + s, 6 + core)
        source = o.at[s, pl.ds(16 * target, 16)]
        return source, out_ref.at[m, k]

    def spread(s, carry):
        which = jnp.where(is_owner, 0, s)
        block = x[s, :, :CHUNK]
        result = times(q[which], block).astype(bf16)
        o[s, :MAIN, :CHUNK] = result[:MAIN]
        stacked = jnp.concatenate(
            [result[MAIN:, 128 * g : 128 * (g + 1)] for g in range(PIECES)]
            + [jnp.zeros((64, 128), bf16)], axis=0)
        o[s, :MAIN, CHUNK:] = lax.dot_general(
            perm[...], stacked, (((0,), (0,)), ((), ())), preferred_element_type=f32).astype(bf16)

        def give(i, carry):
            place, other_core = lax.rem(i, 16), i // 16
            tx = lax.rem(cx + lut(place, [v[0] for v in STEPS]), 4)
            tz = lax.rem(cz + lut(place, [v[1] for v in STEPS]), 4)
            target = 8 * tx + 2 * tz + lax.rem(core + other_core, 2)
            source, dest = outgoing(s, target)
            pltpu.make_async_remote_copy(
                source, dest, o_send, o_recv, device_id=(target, expert), device_id_type=MESH).start()
            return carry

        lax.fori_loop(1, N_ZERO, give, 0)
        source, dest = outgoing(s, zero)
        pltpu.make_async_copy(source, dest, o_recv).start()
        return carry

    lax.fori_loop(0, 3, spread, 0)

    def drain(m, carry):
        to_twin(m).wait_send()
        to_up(m).wait_send()
        forward(m).wait_send()
        keep(m).wait()
        return carry

    lax.fori_loop(0, MATS_GRP, drain, 0)

    @pl.when(is_owner)
    def _():
        poly_to_hub().wait_send()

    sent = x.at[:, pl.ds(0, 16 * (N_ZERO - 1))]
    pltpu.make_async_copy(sent, sent, a_send).wait()
    pltpu.make_async_copy(sent, sent, o_send).wait()
    pltpu.make_async_copy(out_ref, out_ref, o_recv).wait()


def end_kernel(flags, back, live, grad, mom, new_ref, update_ref):
    lost = flags[0]
    stale = beta * (1.0 - lost)
    fresh = beta * lost
    for k in range(CHUNKS):
        span = pl.ds(CHUNK * k, CHUNK)
        update_ref[0, :16, span] = back[0, k, :, :CHUNK]
        update_ref[0, 16:, span] = unpack_rest(back[0, k, :, CHUNK:].astype(f32)).astype(bf16)
        new_ref[0, :16, span] = (
            grad[0, :16, span].astype(f32) + stale * mom[0, :16, span]
            + fresh * live[0, k, :, :CHUNK].astype(f32))
        new_ref[0, 16:, span] = (
            grad[0, 16:, span].astype(f32) + stale * mom[0, 16:, span]
            + fresh * unpack_rest(live[0, k, :, CHUNK:].astype(f32)))


def local(grad, momentum, backup, recovery):
    zero, expert = lax.axis_index("zero"), lax.axis_index("expert")
    lost = zero == recovery[expert]
    mirror = zero == recovery[lax.rem(expert + 1, N_EXPERT)]
    flags = jnp.stack([lost, mirror]).astype(f32)
    whole = (MATS_GRP, CHUNKS, 16, UNIT)
    halves = (MATS_GRP, CHUNKS // 2, 16, UNIT)
    shard = (MATS_GRP, ROWS_DEV, MODEL_WIDTH)
    anywhere = pl.BlockSpec(memory_space=pl.ANY)
    scalars = pl.BlockSpec(memory_space=pltpu.SMEM)
    dma = pltpu.SemaphoreType.DMA
    returned, live = pl.pallas_call(
        main_kernel,
        out_shape=[jax.ShapeDtypeStruct(whole, bf16)] * 2,
        in_specs=[scalars] + [anywhere] * 3,
        out_specs=[anywhere] * 2,
        scratch_shapes=[
            pltpu.VMEM(shard, bf16), pltpu.VMEM(shard, f32), pltpu.VMEM(shard, f32),
            pltpu.VMEM(whole, bf16), pltpu.VMEM(halves, bf16), pltpu.VMEM(halves, bf16),
            pltpu.VMEM(whole, bf16), pltpu.VMEM(whole, bf16),
            pltpu.VMEM((3, R, UNIT), bf16), pltpu.VMEM((3, MAIN, UNIT), bf16),
            pltpu.VMEM((MAIN, MAIN), bf16),
            pltpu.VMEM((3, R, R), f32), pltpu.VMEM((3, R, R), bf16), pltpu.VMEM((R, R), f32),
            pltpu.VMEM((3, HALF, R), bf16), pltpu.VMEM((R, R), bf16), pltpu.VMEM((3, R, R), bf16),
            pltpu.VMEM((R, R), bf16), pltpu.VMEM((R, R), bf16),
            pltpu.VMEM((R, R), bf16), pltpu.VMEM((R, R), bf16),
            dma((3, MATS_GRP)), dma((MATS_GRP,)), dma((MATS_GRP,)), dma((MATS_GRP,)),
            dma((MATS_GRP,)), dma((MATS_GRP,)), dma((MATS_GRP,)), dma, dma, dma((MATS_GRP,)),
            dma, dma, dma, dma, dma((3,)), dma, dma((3,)), dma((3,)), dma((1,)), dma((3,)), dma, dma,
        ],
        compiler_params=pltpu.CompilerParams(
            collective_id=0, has_side_effects=True, vmem_limit_bytes=60 << 20),
    )(flags, grad, momentum, backup)

    def unit_spec():
        return pl.BlockSpec((1, CHUNKS, 16, UNIT), lambda m: (m, 0, 0, 0))

    def shard_spec():
        return pl.BlockSpec((1, ROWS_DEV, MODEL_WIDTH), lambda m: (m, 0, 0))

    return pl.pallas_call(
        end_kernel,
        grid=(MATS_GRP,),
        out_shape=[jax.ShapeDtypeStruct(shard, f32), jax.ShapeDtypeStruct(shard, bf16)],
        in_specs=[scalars, unit_spec(), unit_spec(), shard_spec(), shard_spec()],
        out_specs=[shard_spec(), shard_spec()],
        compiler_params=pltpu.CompilerParams(vmem_limit_bytes=40 << 20),
    )(flags, returned, live, grad, momentum)


def solution(mesh):
    spread = P("expert", "zero", None)
    return jax.shard_map(
        local, mesh=mesh, in_specs=(spread, spread, spread, P()), out_specs=(spread, spread),
        check_vma=False)
```

```python
import jax
import jax.numpy as jnp
from jax import lax
from jax.experimental import pallas as pl
from jax.experimental.pallas import tpu as pltpu
from jax.sharding import PartitionSpec as P

MODEL_WIDTH = 7168
R = 576
MATS_GRP = 12
ROWS_DEV = 18
N_ZERO = 32
N_EXPERT = 4

beta = 0.95
coef_a = 3.4445
coef_b = -4.775
coef_c = 2.0315
eps = 1e-07
SCALE = 0.2 * max(R, MODEL_WIDTH) ** 0.5

CHUNKS = 8
CHUNK = MODEL_WIDTH // CHUNKS
PIECES = CHUNK // 128
UNIT = CHUNK + 128
MAIN = 16 * N_ZERO
HALF = R // 2

CHIP_OF = (0, 2, 5, 1, 3, 11, 6, 7, 4, 12, 9, 8, 13, 15, 10, 14)
TARGET_OF = tuple(CHIP_OF.index(chip) for chip in range(16))
OWNED = 6 * CHUNK

STEPS = ((0, 0), (1, 0), (0, 1), (3, 0), (0, 3), (2, 0), (0, 2), (1, 1),
         (3, 3), (1, 3), (3, 1), (2, 1), (1, 2), (2, 3), (3, 2), (2, 2))
FAR_FIRST = STEPS[:0:-1] + STEPS[:1]
EVEN_STEPS = tuple(v for v in STEPS if sum(v) % 2 == 0)
ODD_STEPS = tuple(v for v in STEPS if sum(v) % 2 == 1)


def order_of(chip):
    x, z = chip // 4, chip % 4
    return [TARGET_OF[4 * ((x + dx) % 4) + (z + dz) % 4] for dx, dz in FAR_FIRST]


CODES = tuple(
    tuple(sum(order_of(chip)[4 * part + i] * 16 ** i for i in range(4)) for chip in range(16))
    for part in range(4))

JOIN, LIFT, SEND = 1, 3, 4

MESH = pl.DeviceIdType.MESH
f32 = jnp.float32
bf16 = jnp.bfloat16


def lut(index, table):
    value = jnp.int32(table[0])
    for place, entry in enumerate(table):
        if place:
            value = jnp.where(index == place, jnp.int32(entry), value)
    return value


def pack_rest(rest):
    pieces = [rest[:, 128 * g : 128 * (g + 1)] for g in range(PIECES)]
    return jnp.concatenate(pieces + [jnp.zeros((2, 128), rest.dtype)], axis=0)


def unpack_rest(tile):
    return jnp.concatenate([tile[2 * g : 2 * g + 2] for g in range(PIECES)], axis=1)


def times(left, right):
    return jnp.dot(left, right, preferred_element_type=f32)


def main_kernel(
    recovery, grad, mom, back, out_ref, live_ref, lost_ref,
    gv, mv, bv, own, other, joined, shifted, units, x, o, perm, gram, gsend, gpeer, ghalf, gin, q,
    ma, mb, mc, md,
    in_sem, d_send, d_recv, y_send, y_recv, f_send, f_recv, a_send, a_recv, v_sem,
    g_send, g_recv, h_send, h_recv, k_send, k_recv, i_send, i_recv, q_send, q_recv, p_send, p_recv,
    o_send, o_recv,
):
    zero, expert = lax.axis_index("zero"), lax.axis_index("expert")
    core = lax.rem(zero, 2)
    chip = zero // 2
    cx, cz = chip // 4, lax.rem(chip, 4)
    parity = lax.rem(cx + cz, 2)
    me = lut(chip, TARGET_OF)
    team, spot = me // 4, lax.rem(me, 4)
    is_owner = spot < 3
    is_hub = spot == 3
    twin = zero + 1 - 2 * core
    up = lax.rem(expert + 1, N_EXPERT)
    down = lax.rem(expert + N_EXPERT - 1, N_EXPERT)
    my_rows = pl.ds(16 * (16 * core + 8 * parity + 2 * cx + cz // 2), 16)
    lost = jnp.where(recovery[expert] == zero, 1.0, 0.0)
    mirror = jnp.where(recovery[up] == zero, 1.0, 0.0)
    lost_ref[0] = jnp.where(recovery[expert] == zero, 1, 0)

    barrier = pltpu.get_barrier_semaphore()

    def greet(i, carry):
        pl.semaphore_signal(
            barrier, inc=1, device_id=(lax.rem(zero + i, N_ZERO), expert), device_id_type=MESH)
        return carry

    lax.fori_loop(1, N_ZERO, greet, 0)
    pl.semaphore_signal(barrier, inc=1, device_id=(zero, up), device_id_type=MESH)
    pl.semaphore_signal(barrier, inc=1, device_id=(zero, down), device_id_type=MESH)

    codes = [lut(chip, table) for table in CODES]

    def next_target(i, code):
        fresh = jnp.where(
            i < 4, codes[0], jnp.where(i < 8, codes[1], jnp.where(i < 12, codes[2], codes[3])))
        code = jnp.where(lax.rem(i, 4) == 0, fresh, code // 16)
        return lax.rem(code, 16), code

    def loads(target, source, dest, sem, act):
        t, place = target // 4, lax.rem(target, 4)

        @pl.when(place < 3)
        def _():
            part = (3 * t + place, slice(None), pl.ds(0, OWNED))
            act(pltpu.make_async_copy(source.at[part], dest.at[part], sem))

        @pl.when(place == 3)
        def _():
            part = (pl.ds(3 * t, 3), slice(None), pl.ds(OWNED, MODEL_WIDTH - OWNED))
            act(pltpu.make_async_copy(source.at[part], dest.at[part], sem))

    def back_loads(target, act):
        loads(target, back, bv, in_sem.at[0, target], act)

    def grad_loads(target, act):
        loads(target, grad, gv, in_sem.at[1, target], act)

    def mom_loads(target, act):
        loads(target, mom, mv, in_sem.at[2, target], act)

    def begin(copy):
        copy.start()

    def finish(copy):
        copy.wait()

    def load(i, code):
        target, code = next_target(i, code)
        back_loads(target, begin)
        grad_loads(target, begin)
        mom_loads(target, begin)
        return code

    lax.fori_loop(0, 16, load, jnp.int32(0))

    def sources(target, u):
        t, place = target // 4, lax.rem(target, 4)
        c, s = u // 3, u % 3
        m = 3 * t + jnp.where(place < 3, place, s)
        k = jnp.where(place < 3, 3 * c + s, 6 + c)
        return c, s, m, pl.ds(pl.multiple_of(k * CHUNK, 128), CHUNK)

    def make_own(target):
        back_loads(target, finish)
        for u in range(6):
            c, s, m, span = sources(target, u)
            own[target, c, s, :, :CHUNK] = (bv[m, :16, span] * mirror).astype(bf16)
            own[target, c, s, :, CHUNK:] = pack_rest(bv[m, 16:, span] * mirror).astype(bf16)

    def make_units(target):
        grad_loads(target, finish)
        mom_loads(target, finish)
        stale = (beta * beta) * (1.0 - lost)
        fresh = (beta * beta) * lost
        for u in range(6):
            c, s, m, span = sources(target, u)
            top = (1.0 + beta) * gv[m, :16, span].astype(f32) + stale * mv[m, :16, span]
            units[target, c, s, :, :CHUNK] = (
                top + fresh * shifted[target, c, s, :, :CHUNK].astype(f32)).astype(bf16)
            rest = (1.0 + beta) * gv[m, 16:, span].astype(f32) + stale * mv[m, 16:, span]
            units[target, c, s, :, CHUNK:] = (
                pack_rest(rest) + fresh * shifted[target, c, s, :, CHUNK:].astype(f32)).astype(bf16)

    rows = lax.broadcasted_iota(jnp.int32, (MAIN, MAIN), 0)
    cols = lax.broadcasted_iota(jnp.int32, (MAIN, MAIN), 1)
    wanted = 16 * (lax.rem(rows, 64) // 2) + 2 * (rows // 64) + lax.rem(rows, 2)
    perm[...] = jnp.where(cols == wanted, 1.0, 0.0).astype(bf16)

    first, first_code = next_target(jnp.int32(0), jnp.int32(0))
    make_own(first)

    pl.semaphore_wait(barrier, N_ZERO + 1)

    def to_twin(n):
        return pltpu.make_async_remote_copy(
            own.at[n, 1 - core], other.at[n], d_send.at[n], d_recv.at[n],
            device_id=(twin, expert), device_id_type=MESH)

    def to_up(n):
        return pltpu.make_async_remote_copy(
            joined.at[n], shifted.at[n, core], y_send.at[n], y_recv.at[n],
            device_id=(zero, up), device_id_type=MESH)

    def forward(n):
        return pltpu.make_async_remote_copy(
            shifted.at[n, core], shifted.at[n, core], f_send.at[n], f_recv.at[n],
            device_id=(twin, expert), device_id_type=MESH)

    def keep(n):
        return pltpu.make_async_copy(shifted.at[n], live_ref.at[n], v_sem.at[n])

    def deliver(source, target):
        place = x.at[:, my_rows]

        @pl.when(target != zero)
        def _():
            pltpu.make_async_remote_copy(
                source, place, a_send, a_recv, device_id=(target, expert), device_id_type=MESH).start()

        @pl.when(target == zero)
        def _():
            pltpu.make_async_copy(source, place, a_recv).start()

    def gather_rest():
        pltpu.make_async_copy(x.at[:, pl.ds(0, MAIN)], x.at[:, pl.ds(0, MAIN)], a_recv).wait()
        packed = jnp.concatenate([x[s, :MAIN, CHUNK:] for s in range(3)], axis=1)
        rest = times(perm[...], packed).astype(bf16)
        for s in range(3):
            for g in range(PIECES):
                x[s, MAIN:, 128 * g : 128 * (g + 1)] = (
                    rest[64 * g : 64 * (g + 1), 128 * s : 128 * (s + 1)])

    def gram_of(s):
        block = x[s, :, :CHUNK]
        return lax.dot_general(block, block, (((1,), (1,)), ((), ())), preferred_element_type=f32)

    my_half = pl.ds(HALF * core, HALF)
    their_half = pl.ds(HALF - HALF * core, HALF)

    def hub_to_twin(s):
        return pltpu.make_async_remote_copy(
            gsend.at[s, their_half], ghalf.at[s], h_send.at[s], h_recv.at[s],
            device_id=(twin, expert), device_id_type=MESH)

    def hub_to_owner(s):
        return pltpu.make_async_remote_copy(
            ghalf.at[s], gin.at[my_half], k_send.at[s], k_recv,
            device_id=(2 * lut(4 * team + s, CHIP_OF) + core, expert), device_id_type=MESH)

    def stage(i, carry):
        code, past = carry[0], carry[1:]
        now = past[0]

        @pl.when(i < 16)
        def _():
            to_twin(now).start()

        @pl.when(jnp.logical_and(i >= JOIN, i < 16 + JOIN))
        def _():
            to_twin(past[JOIN]).wait_recv()
            joined[past[JOIN]] = own[past[JOIN], core] + other[past[JOIN]]
            to_up(past[JOIN]).start()

        @pl.when(jnp.logical_and(i >= LIFT, i < 16 + LIFT))
        def _():
            to_up(past[LIFT]).wait_recv()
            forward(past[LIFT]).start()

        @pl.when(i >= SEND)
        def _():
            forward(past[SEND]).wait_recv()
            keep(past[SEND]).start()
            make_units(past[SEND])
            for c in range(2):
                deliver(units.at[past[SEND], c], 2 * lut(past[SEND], CHIP_OF) + c)

        later, code = next_target(i + 1, code)

        @pl.when(i + 1 < 16)
        def _():
            make_own(later)

        return (code, later) + past[:SEND]

    lax.fori_loop(0, 16 + SEND, stage, (first_code, first) + (jnp.int32(0),) * SEND)

    def gram_to_twin():
        return pltpu.make_async_remote_copy(
            gram.at[0], gpeer, g_send, g_recv, device_id=(twin, expert), device_id_type=MESH)

    def half_to_twin():
        return pltpu.make_async_remote_copy(
            gin.at[my_half], gin.at[my_half], i_send, i_recv,
            device_id=(twin, expert), device_id_type=MESH)

    def part_rows(n):
        return pl.ds(MAIN + 32 * core, 32) if n == 0 else pl.ds(128 * (n - 1) + 64 * core, 64)

    def poly_to_hub(n):
        return pltpu.make_async_remote_copy(
            q.at[0, part_rows(n)], q.at[spot, part_rows(n)], p_send.at[n], p_recv.at[spot, n],
            device_id=(2 * lut(4 * team + 3, CHIP_OF) + core, expert), device_id_type=MESH)

    def poly_to_twin(s, n):
        return pltpu.make_async_remote_copy(
            q.at[s, part_rows(n)], q.at[s, part_rows(n)], q_send.at[s, n], q_recv.at[s, n],
            device_id=(twin, expert), device_id_type=MESH)

    gather_rest()

    @pl.when(is_hub)
    def _():
        for s in range(3):
            part = gram_of(s)
            gram[s] = part
            gsend[s] = part.astype(bf16)
            hub_to_twin(s).start()
        for s in range(3):
            hub_to_twin(s).wait_recv()
            ghalf[s] = (gram[s, my_half] + ghalf[s].astype(f32)).astype(bf16)
            hub_to_owner(s).start()

    @pl.when(is_owner)
    def _():
        gram[0] = gram_of(0) + gram_of(1) + gram_of(2)
        gram_to_twin().start()
        pltpu.make_async_copy(gin.at[my_half], gin.at[my_half], k_recv).wait()
        half_to_twin().start()
        gram_to_twin().wait()
        total = gram[0] + gpeer[...]
        half_to_twin().wait()
        total = total + gin[...].astype(f32)
        eye = (lax.broadcasted_iota(jnp.int32, (R, R), 0)
               == lax.broadcasted_iota(jnp.int32, (R, R), 1))
        norm = jnp.sqrt(jnp.sum(jnp.where(eye, total, 0.0)))
        inverse = 1.0 / (norm + eps)
        a, b, c = coef_a, coef_b, coef_c
        ga = total * (inverse * inverse)
        ma[...] = ga.astype(bf16)
        gram[0] = ga
        d1 = b * gram[0] + c * times(ma[...], ma[...])
        gram[1] = d1
        mb[...] = d1.astype(bf16)
        mc[...] = (2.0 * a * gram[1] + times(mb[...], mb[...])).astype(bf16)
        a1 = a * a * gram[0] + times(ma[...], mc[...])
        gram[0] = a1
        ma[...] = a1.astype(bf16)
        d2 = b * gram[0] + c * times(ma[...], ma[...])
        gram[2] = d2
        mc[...] = d2.astype(bf16)
        gram[1] = a * (gram[1] + gram[2]) + times(mb[...], mc[...])
        md[...] = (2.0 * a * gram[2] + times(mc[...], mc[...])).astype(bf16)
        a2 = a * a * gram[0] + times(ma[...], md[...])
        gram[0] = a2
        ma[...] = a2.astype(bf16)
        d3 = b * gram[0] + c * times(ma[...], ma[...])
        gram[2] = d3
        mb[...] = d3.astype(bf16)
        mc[...] = gram[1].astype(bf16)
        poly = a * gram[1] + a * a * gram[2] + times(mc[...], mb[...])
        poly = jnp.where(eye, poly + a * a * a, poly)
        q[0] = (poly * (inverse * SCALE)).astype(bf16)
        for n in range(5):
            poly_to_hub(n).start()

    def arrive(n):
        @pl.when(is_hub)
        def _():
            for s in range(3):
                pltpu.make_async_copy(
                    q.at[s, part_rows(n)], q.at[s, part_rows(n)], p_recv.at[s, n]).wait()
                poly_to_twin(s, n).start()
            for s in range(3):
                poly_to_twin(s, n).wait_recv()

    def apply(s, rows):
        which = jnp.where(is_owner, 0, s)
        return times(q[which, rows], x[s, :, :CHUNK]).astype(bf16)

    arrive(0)
    for s in range(3):
        rest = apply(s, pl.ds(MAIN, R - MAIN))
        stacked = jnp.concatenate(
            [rest[:, 128 * g : 128 * (g + 1)] for g in range(PIECES)]
            + [jnp.zeros((64, 128), bf16)], axis=0)
        o[s, :, CHUNK:] = lax.dot_general(
            perm[...], stacked, (((0,), (0,)), ((), ())), preferred_element_type=f32).astype(bf16)

    for n in range(4):
        arrive(n + 1)
        for s in range(3):
            o[s, 128 * n : 128 * (n + 1), :CHUNK] = apply(s, pl.ds(128 * n, 128))
        to_core, to_parity = n // 2, n % 2
        odd = parity != to_parity

        def give(i, carry):
            tx = lax.rem(cx + lut(jnp.where(odd, i + 8, i), [v[0] for v in EVEN_STEPS + ODD_STEPS]), 4)
            tz = lax.rem(cz + lut(jnp.where(odd, i + 8, i), [v[1] for v in EVEN_STEPS + ODD_STEPS]), 4)
            target = 8 * tx + 2 * tz + to_core
            source = o.at[:, pl.ds(128 * n + 16 * (2 * tx + tz // 2), 16)]

            @pl.when(target != zero)
            def _():
                pltpu.make_async_remote_copy(
                    source, out_ref.at[me, core], o_send, o_recv,
                    device_id=(target, expert), device_id_type=MESH).start()

            @pl.when(target == zero)
            def _():
                pltpu.make_async_copy(source, out_ref.at[me, core], o_recv).start()

            return carry

        lax.fori_loop(0, 8, give, 0)

    def drain(n, carry):
        to_twin(n).wait_send()
        to_up(n).wait_send()
        forward(n).wait_send()
        keep(n).wait()
        return carry

    lax.fori_loop(0, 16, drain, 0)

    @pl.when(is_owner)
    def _():
        for n in range(5):
            poly_to_hub(n).wait_send()

    @pl.when(is_hub)
    def _():
        for s in range(3):
            hub_to_twin(s).wait_send()
            hub_to_owner(s).wait_send()
            for n in range(5):
                poly_to_twin(s, n).wait_send()

    sent = x.at[:, pl.ds(0, 16 * (N_ZERO - 1))]
    pltpu.make_async_copy(sent, sent, a_send).wait()
    pltpu.make_async_copy(sent, sent, o_send).wait()
    pltpu.make_async_copy(out_ref, out_ref, o_recv).wait()


def end_kernel(lost_ref, back, back_hub, live, live_hub, grad, mom, new_ref, update_ref):
    lost = lost_ref[0].astype(f32)
    stale = beta * (1.0 - lost)
    fresh = beta * lost
    for k in range(CHUNKS):
        span = pl.ds(CHUNK * k, CHUNK)
        unit = (0, 0, k // 3, k % 3) if k < 6 else (0, 0, k - 6, 0)
        returned = back if k < 6 else back_hub
        held = live if k < 6 else live_hub
        update_ref[0, :16, span] = returned[unit][:, :CHUNK]
        update_ref[0, 16:, span] = unpack_rest(returned[unit][:, CHUNK:].astype(f32)).astype(bf16)
        new_ref[0, :16, span] = (
            grad[0, :16, span].astype(f32) + stale * mom[0, :16, span]
            + fresh * held[unit][:, :CHUNK].astype(f32))
        new_ref[0, 16:, span] = (
            grad[0, 16:, span].astype(f32) + stale * mom[0, 16:, span]
            + fresh * unpack_rest(held[unit][:, CHUNK:].astype(f32)))


def local(grad, momentum, backup, recovery):
    whole = (16, 2, 3, 16, UNIT)
    halves = (16, 3, 16, UNIT)
    shard = (MATS_GRP, ROWS_DEV, MODEL_WIDTH)
    anywhere = pl.BlockSpec(memory_space=pl.ANY)
    scalars = pl.BlockSpec(memory_space=pltpu.SMEM)
    dma = pltpu.SemaphoreType.DMA
    steps = dma((16,))
    returned, live, lost = pl.pallas_call(
        main_kernel,
        out_shape=[jax.ShapeDtypeStruct(whole, bf16)] * 2 + [jax.ShapeDtypeStruct((1,), jnp.int32)],
        in_specs=[scalars] + [anywhere] * 3,
        out_specs=[anywhere] * 2 + [scalars],
        scratch_shapes=[
            pltpu.VMEM(shard, bf16), pltpu.VMEM(shard, f32), pltpu.VMEM(shard, f32),
            pltpu.VMEM(whole, bf16), pltpu.VMEM(halves, bf16), pltpu.VMEM(halves, bf16),
            pltpu.VMEM(whole, bf16), pltpu.VMEM(whole, bf16),
            pltpu.VMEM((3, R, UNIT), bf16), pltpu.VMEM((3, MAIN, UNIT), bf16),
            pltpu.VMEM((MAIN, MAIN), bf16),
            pltpu.VMEM((3, R, R), f32), pltpu.VMEM((3, R, R), bf16), pltpu.VMEM((R, R), f32),
            pltpu.VMEM((3, HALF, R), bf16), pltpu.VMEM((R, R), bf16), pltpu.VMEM((3, R, R), bf16),
            pltpu.VMEM((R, R), bf16), pltpu.VMEM((R, R), bf16),
            pltpu.VMEM((R, R), bf16), pltpu.VMEM((R, R), bf16),
            dma((3, 16)), steps, steps, steps, steps, steps, steps, dma, dma, steps,
            dma, dma, dma((3,)), dma((3,)), dma((3,)), dma, dma, dma,
            dma((3, 5)), dma((3, 5)), dma((5,)), dma((3, 5)), dma, dma,
        ],
        compiler_params=pltpu.CompilerParams(
            collective_id=0, has_side_effects=True, vmem_limit_bytes=60 << 20),
    )(recovery, grad, momentum, backup)

    def owner_block(m, scale=1):
        return (m // 3 * scale, lax.rem(m, 3) * scale, 0, 0, 0, 0)

    def hub_block(m, scale=1):
        return (m // 3 * scale, 3, 0, lax.rem(m, 3) * scale, 0, 0)

    owner_shape, hub_shape = (1, 1, 2, 3, 16, UNIT), (1, 1, 2, 1, 16, UNIT)
    plain = pl.BlockSpec((1, ROWS_DEV, MODEL_WIDTH), lambda m, lost: (m, 0, 0))
    parted = (4, 4, 2, 3, 16, UNIT)
    return pl.pallas_call(
        end_kernel,
        grid_spec=pltpu.PrefetchScalarGridSpec(
            num_scalar_prefetch=1,
            grid=(MATS_GRP,),
            in_specs=[
                pl.BlockSpec(owner_shape, lambda m, lost: owner_block(m)),
                pl.BlockSpec(hub_shape, lambda m, lost: hub_block(m)),
                pl.BlockSpec(owner_shape, lambda m, lost: owner_block(m, lost[0])),
                pl.BlockSpec(hub_shape, lambda m, lost: hub_block(m, lost[0])),
                plain,
                pl.BlockSpec((1, ROWS_DEV, MODEL_WIDTH), lambda m, lost: (m * (1 - lost[0]), 0, 0)),
            ],
            out_specs=[plain, plain],
        ),
        out_shape=[jax.ShapeDtypeStruct(shard, f32), jax.ShapeDtypeStruct(shard, bf16)],
        compiler_params=pltpu.CompilerParams(vmem_limit_bytes=60 << 20),
    )(lost, returned.reshape(parted), returned.reshape(parted), live.reshape(parted),
      live.reshape(parted), grad, momentum)


def solution(mesh):
    spread = P("expert", "zero", None)
    return jax.shard_map(
        local, mesh=mesh, in_specs=(spread, spread, spread, P()), out_specs=(spread, spread),
        check_vma=False)
```

```python
import jax
import jax.numpy as jnp
from jax import lax
from jax.experimental import pallas as pl
from jax.experimental.pallas import tpu as pltpu
from jax.sharding import PartitionSpec as P

MODEL_WIDTH = 7168
R = 576
MATS_GRP = 12
ROWS_DEV = 18
N_ZERO = 32
N_EXPERT = 4

beta = 0.95
coef_a = 3.4445
coef_b = -4.775
coef_c = 2.0315
eps = 1e-07
SCALE = 0.2 * max(R, MODEL_WIDTH) ** 0.5

CHUNKS = 8
CHUNK = MODEL_WIDTH // CHUNKS
PIECES = CHUNK // 128
UNIT = CHUNK + 128
MAIN = 16 * N_ZERO
HALF = R // 2

CHIP_OF = (0, 2, 5, 1, 3, 11, 6, 7, 4, 12, 9, 8, 13, 15, 10, 14)
TARGET_OF = tuple(CHIP_OF.index(chip) for chip in range(16))
OWNED = 6 * CHUNK

STEPS = ((0, 0), (1, 0), (0, 1), (3, 0), (0, 3), (2, 0), (0, 2), (1, 1),
         (3, 3), (1, 3), (3, 1), (2, 1), (1, 2), (2, 3), (3, 2), (2, 2))
FAR_FIRST = STEPS[:0:-1] + STEPS[:1]
EVEN_STEPS = tuple(v for v in STEPS if sum(v) % 2 == 0)
ODD_STEPS = tuple(v for v in STEPS if sum(v) % 2 == 1)
HUBS_BEFORE = 8


def order_of(chip):
    x, z = chip // 4, chip % 4
    turns = [TARGET_OF[4 * ((x + dx) % 4) + (z + dz) % 4] for dx, dz in FAR_FIRST]
    for late in range(HUBS_BEFORE, 16):
        if turns[late] % 4 == 3:
            early = max(i for i in range(HUBS_BEFORE) if turns[i] % 4 != 3)
            turns[late], turns[early] = turns[early], turns[late]
    return turns


CODES = tuple(
    tuple(sum(order_of(chip)[4 * part + i] * 16 ** i for i in range(4)) for chip in range(16))
    for part in range(4))

JOIN, LIFT, SEND = 1, 3, 4

MESH = pl.DeviceIdType.MESH
f32 = jnp.float32
bf16 = jnp.bfloat16


def lut(index, table):
    value = jnp.int32(table[0])
    for place, entry in enumerate(table):
        if place:
            value = jnp.where(index == place, jnp.int32(entry), value)
    return value


def pack_rest(rest):
    pieces = [rest[:, 128 * g : 128 * (g + 1)] for g in range(PIECES)]
    return jnp.concatenate(pieces + [jnp.zeros((2, 128), rest.dtype)], axis=0)


def unpack_rest(tile):
    return jnp.concatenate([tile[2 * g : 2 * g + 2] for g in range(PIECES)], axis=1)


def times(left, right):
    return jnp.dot(left, right, preferred_element_type=f32)


def main_kernel(
    recovery, grad, mom, back, out_ref, live_ref, lost_ref,
    gv, mv, bv, own, other, joined, shifted, units, x, o, perm, gram, gsend, gpeer, ghalf, gin, q,
    ma, mb, mc, md,
    in_sem, d_send, d_recv, y_send, y_recv, f_send, f_recv, a_send, a_recv, v_sem,
    g_send, g_recv, h_send, h_recv, k_send, k_recv, i_send, i_recv, q_send, q_recv, p_send, p_recv,
    o_send, o_recv,
):
    zero, expert = lax.axis_index("zero"), lax.axis_index("expert")
    core = lax.rem(zero, 2)
    chip = zero // 2
    cx, cz = chip // 4, lax.rem(chip, 4)
    parity = lax.rem(cx + cz, 2)
    me = lut(chip, TARGET_OF)
    team, spot = me // 4, lax.rem(me, 4)
    is_owner = spot < 3
    is_hub = spot == 3
    twin = zero + 1 - 2 * core
    up = lax.rem(expert + 1, N_EXPERT)
    down = lax.rem(expert + N_EXPERT - 1, N_EXPERT)
    my_rows = pl.ds(16 * (16 * core + 8 * parity + 2 * cx + cz // 2), 16)
    lost = jnp.where(recovery[expert] == zero, 1.0, 0.0)
    mirror = jnp.where(recovery[up] == zero, 1.0, 0.0)
    lost_ref[0] = jnp.where(recovery[expert] == zero, 1, 0)

    barrier = pltpu.get_barrier_semaphore()

    def greet(i, carry):
        pl.semaphore_signal(
            barrier, inc=1, device_id=(lax.rem(zero + i, N_ZERO), expert), device_id_type=MESH)
        return carry

    lax.fori_loop(1, N_ZERO, greet, 0)
    pl.semaphore_signal(barrier, inc=1, device_id=(zero, up), device_id_type=MESH)
    pl.semaphore_signal(barrier, inc=1, device_id=(zero, down), device_id_type=MESH)

    codes = [lut(chip, table) for table in CODES]

    def next_target(i, code):
        fresh = jnp.where(
            i < 4, codes[0], jnp.where(i < 8, codes[1], jnp.where(i < 12, codes[2], codes[3])))
        code = jnp.where(lax.rem(i, 4) == 0, fresh, code // 16)
        return lax.rem(code, 16), code

    def loads(target, source, dest, sem, act):
        t, place = target // 4, lax.rem(target, 4)

        @pl.when(place < 3)
        def _():
            part = (3 * t + place, slice(None), pl.ds(0, OWNED))
            act(pltpu.make_async_copy(source.at[part], dest.at[part], sem))

        @pl.when(place == 3)
        def _():
            part = (pl.ds(3 * t, 3), slice(None), pl.ds(OWNED, MODEL_WIDTH - OWNED))
            act(pltpu.make_async_copy(source.at[part], dest.at[part], sem))

    def back_loads(target, act):
        loads(target, back, bv, in_sem.at[0, target], act)

    def grad_loads(target, act):
        loads(target, grad, gv, in_sem.at[1, target], act)

    def mom_loads(target, act):
        loads(target, mom, mv, in_sem.at[2, target], act)

    def begin(copy):
        copy.start()

    def finish(copy):
        copy.wait()

    def load(i, code):
        target, code = next_target(i, code)
        back_loads(target, begin)
        grad_loads(target, begin)
        mom_loads(target, begin)
        return code

    lax.fori_loop(0, 16, load, jnp.int32(0))

    def sources(target, u):
        t, place = target // 4, lax.rem(target, 4)
        c, s = u // 3, u % 3
        m = 3 * t + jnp.where(place < 3, place, s)
        k = jnp.where(place < 3, 3 * c + s, 6 + c)
        return c, s, m, pl.ds(pl.multiple_of(k * CHUNK, 128), CHUNK)

    def make_own(target):
        back_loads(target, finish)
        for u in range(6):
            c, s, m, span = sources(target, u)
            own[target, c, s, :, :CHUNK] = (bv[m, :16, span] * mirror).astype(bf16)
            own[target, c, s, :, CHUNK:] = pack_rest(bv[m, 16:, span] * mirror).astype(bf16)

    def make_units(target):
        grad_loads(target, finish)
        mom_loads(target, finish)
        stale = (beta * beta) * (1.0 - lost)
        fresh = (beta * beta) * lost
        for u in range(6):
            c, s, m, span = sources(target, u)
            top = (1.0 + beta) * gv[m, :16, span].astype(f32) + stale * mv[m, :16, span]
            units[target, c, s, :, :CHUNK] = (
                top + fresh * shifted[target, c, s, :, :CHUNK].astype(f32)).astype(bf16)
            rest = (1.0 + beta) * gv[m, 16:, span].astype(f32) + stale * mv[m, 16:, span]
            units[target, c, s, :, CHUNK:] = (
                pack_rest(rest) + fresh * shifted[target, c, s, :, CHUNK:].astype(f32)).astype(bf16)

    rows = lax.broadcasted_iota(jnp.int32, (MAIN, MAIN), 0)
    cols = lax.broadcasted_iota(jnp.int32, (MAIN, MAIN), 1)
    wanted = 16 * (lax.rem(rows, 64) // 2) + 2 * (rows // 64) + lax.rem(rows, 2)
    perm[...] = jnp.where(cols == wanted, 1.0, 0.0).astype(bf16)

    first, first_code = next_target(jnp.int32(0), jnp.int32(0))
    make_own(first)

    pl.semaphore_wait(barrier, N_ZERO + 1)

    def to_twin(n):
        return pltpu.make_async_remote_copy(
            own.at[n, 1 - core], other.at[n], d_send.at[n], d_recv.at[n],
            device_id=(twin, expert), device_id_type=MESH)

    def to_up(n):
        return pltpu.make_async_remote_copy(
            joined.at[n], shifted.at[n, core], y_send.at[n], y_recv.at[n],
            device_id=(zero, up), device_id_type=MESH)

    def forward(n):
        return pltpu.make_async_remote_copy(
            shifted.at[n, core], shifted.at[n, core], f_send.at[n], f_recv.at[n],
            device_id=(twin, expert), device_id_type=MESH)

    def keep(n):
        return pltpu.make_async_copy(shifted.at[n], live_ref.at[n], v_sem.at[n])

    def deliver(source, target):
        place = x.at[:, my_rows]

        @pl.when(target != zero)
        def _():
            pltpu.make_async_remote_copy(
                source, place, a_send, a_recv, device_id=(target, expert), device_id_type=MESH).start()

        @pl.when(target == zero)
        def _():
            pltpu.make_async_copy(source, place, a_recv).start()

    def gather_rest():
        pltpu.make_async_copy(x.at[:, pl.ds(0, MAIN)], x.at[:, pl.ds(0, MAIN)], a_recv).wait()
        packed = jnp.concatenate([x[s, :MAIN, CHUNK:] for s in range(3)], axis=1)
        rest = times(perm[...], packed).astype(bf16)
        for s in range(3):
            for g in range(PIECES):
                x[s, MAIN:, 128 * g : 128 * (g + 1)] = (
                    rest[64 * g : 64 * (g + 1), 128 * s : 128 * (s + 1)])

    def gram_of(s, rows=slice(None)):
        return lax.dot_general(
            x[s, rows, :CHUNK], x[s, :, :CHUNK], (((1,), (1,)), ((), ())), preferred_element_type=f32)

    my_half = pl.ds(HALF * core, HALF)
    their_half = pl.ds(HALF - HALF * core, HALF)

    def hub_to_twin(s):
        return pltpu.make_async_remote_copy(
            gsend.at[s, their_half], ghalf.at[s], h_send.at[s], h_recv.at[s],
            device_id=(twin, expert), device_id_type=MESH)

    def hub_to_owner(s):
        return pltpu.make_async_remote_copy(
            ghalf.at[s], gin.at[my_half], k_send.at[s], k_recv,
            device_id=(2 * lut(4 * team + s, CHIP_OF) + core, expert), device_id_type=MESH)

    def pass_on(s):
        hub_to_twin(s).wait_recv()
        ghalf[s] = (gram[s, my_half] + ghalf[s].astype(f32)).astype(bf16)
        hub_to_owner(s).start()

    def stage(i, carry):
        code, past = carry[0], carry[1:]
        now = past[0]

        @pl.when(i < 16)
        def _():
            to_twin(now).start()

        @pl.when(jnp.logical_and(i >= JOIN, i < 16 + JOIN))
        def _():
            to_twin(past[JOIN]).wait_recv()
            joined[past[JOIN]] = own[past[JOIN], core] + other[past[JOIN]]
            to_up(past[JOIN]).start()

        @pl.when(jnp.logical_and(i >= LIFT, i < 16 + LIFT))
        def _():
            to_up(past[LIFT]).wait_recv()
            forward(past[LIFT]).start()

        @pl.when(i >= SEND)
        def _():
            forward(past[SEND]).wait_recv()
            keep(past[SEND]).start()
            make_units(past[SEND])
            for c in range(2):
                deliver(units.at[past[SEND], c], 2 * lut(past[SEND], CHIP_OF) + c)

        later, code = next_target(i + 1, code)

        @pl.when(i + 1 < 16)
        def _():
            make_own(later)

        return (code, later) + past[:SEND]

    lax.fori_loop(0, 16 + SEND, stage, (first_code, first) + (jnp.int32(0),) * SEND)

    def gram_to_twin(n):
        rows = pl.ds(HALF * n, HALF)
        return pltpu.make_async_remote_copy(
            gram.at[0, rows], gpeer.at[rows], g_send.at[n], g_recv.at[n],
            device_id=(twin, expert), device_id_type=MESH)

    def half_to_twin():
        return pltpu.make_async_remote_copy(
            gin.at[my_half], gin.at[my_half], i_send, i_recv,
            device_id=(twin, expert), device_id_type=MESH)

    def part_rows(n):
        return pl.ds(MAIN + 32 * core, 32) if n == 0 else pl.ds(128 * (n - 1) + 64 * core, 64)

    def poly_to_hub(n):
        return pltpu.make_async_remote_copy(
            q.at[0, part_rows(n)], q.at[spot, part_rows(n)], p_send.at[n], p_recv.at[spot, n],
            device_id=(2 * lut(4 * team + 3, CHIP_OF) + core, expert), device_id_type=MESH)

    def poly_to_twin(s, n):
        return pltpu.make_async_remote_copy(
            q.at[s, part_rows(n)], q.at[s, part_rows(n)], q_send.at[s, n], q_recv.at[s, n],
            device_id=(twin, expert), device_id_type=MESH)

    gather_rest()

    @pl.when(is_hub)
    def _():
        for s in range(3):
            part = gram_of(s)
            gram[s] = part
            gsend[s] = part.astype(bf16)
            hub_to_twin(s).start()
            if s:
                pass_on(s - 1)
        pass_on(2)

    @pl.when(is_owner)
    def _():
        for n in range(2):
            rows = slice(HALF * n, HALF * (n + 1))
            gram[0, rows] = gram_of(0, rows) + gram_of(1, rows) + gram_of(2, rows)
            gram_to_twin(n).start()
        pltpu.make_async_copy(gin.at[my_half], gin.at[my_half], k_recv).wait()
        half_to_twin().start()
        gram_to_twin(0).wait()
        gram_to_twin(1).wait()
        total = gram[0] + gpeer[...]
        half_to_twin().wait()
        total = total + gin[...].astype(f32)
        eye = (lax.broadcasted_iota(jnp.int32, (R, R), 0)
               == lax.broadcasted_iota(jnp.int32, (R, R), 1))
        norm = jnp.sqrt(jnp.sum(jnp.where(eye, total, 0.0)))
        inverse = 1.0 / (norm + eps)
        a, b, c = coef_a, coef_b, coef_c
        ga = total * (inverse * inverse)
        ma[...] = ga.astype(bf16)
        gram[0] = ga
        d1 = b * gram[0] + c * times(ma[...], ma[...])
        gram[1] = d1
        mb[...] = d1.astype(bf16)
        mc[...] = (2.0 * a * gram[1] + times(mb[...], mb[...])).astype(bf16)
        a1 = a * a * gram[0] + times(ma[...], mc[...])
        gram[0] = a1
        ma[...] = a1.astype(bf16)
        d2 = b * gram[0] + c * times(ma[...], ma[...])
        gram[2] = d2
        mc[...] = d2.astype(bf16)
        gram[1] = a * (gram[1] + gram[2]) + times(mb[...], mc[...])
        md[...] = (2.0 * a * gram[2] + times(mc[...], mc[...])).astype(bf16)
        a2 = a * a * gram[0] + times(ma[...], md[...])
        gram[0] = a2
        ma[...] = a2.astype(bf16)
        d3 = b * gram[0] + c * times(ma[...], ma[...])
        gram[2] = d3
        mb[...] = d3.astype(bf16)
        mc[...] = gram[1].astype(bf16)
        poly = a * gram[1] + a * a * gram[2] + times(mc[...], mb[...])
        poly = jnp.where(eye, poly + a * a * a, poly)
        q[0] = (poly * (inverse * SCALE)).astype(bf16)
        for n in range(5):
            poly_to_hub(n).start()

    def arrive(n):
        @pl.when(is_hub)
        def _():
            for s in range(3):
                pltpu.make_async_copy(
                    q.at[s, part_rows(n)], q.at[s, part_rows(n)], p_recv.at[s, n]).wait()
                poly_to_twin(s, n).start()
            for s in range(3):
                poly_to_twin(s, n).wait_recv()

    def apply(s, rows):
        which = jnp.where(is_owner, 0, s)
        return times(q[which, rows], x[s, :, :CHUNK]).astype(bf16)

    arrive(0)
    for s in range(3):
        rest = apply(s, pl.ds(MAIN, R - MAIN))
        stacked = jnp.concatenate(
            [rest[:, 128 * g : 128 * (g + 1)] for g in range(PIECES)]
            + [jnp.zeros((64, 128), bf16)], axis=0)
        o[s, :, CHUNK:] = lax.dot_general(
            perm[...], stacked, (((0,), (0,)), ((), ())), preferred_element_type=f32).astype(bf16)

    for n in range(4):
        arrive(n + 1)
        for s in range(3):
            o[s, 128 * n : 128 * (n + 1), :CHUNK] = apply(s, pl.ds(128 * n, 128))
        to_core, to_parity = n // 2, n % 2
        odd = parity != to_parity

        def give(i, carry):
            tx = lax.rem(cx + lut(jnp.where(odd, i + 8, i), [v[0] for v in EVEN_STEPS + ODD_STEPS]), 4)
            tz = lax.rem(cz + lut(jnp.where(odd, i + 8, i), [v[1] for v in EVEN_STEPS + ODD_STEPS]), 4)
            target = 8 * tx + 2 * tz + to_core
            source = o.at[:, pl.ds(128 * n + 16 * (2 * tx + tz // 2), 16)]

            @pl.when(target != zero)
            def _():
                pltpu.make_async_remote_copy(
                    source, out_ref.at[me, core], o_send, o_recv,
                    device_id=(target, expert), device_id_type=MESH).start()

            @pl.when(target == zero)
            def _():
                pltpu.make_async_copy(source, out_ref.at[me, core], o_recv).start()

            return carry

        lax.fori_loop(0, 8, give, 0)

    def drain(n, carry):
        to_twin(n).wait_send()
        to_up(n).wait_send()
        forward(n).wait_send()
        keep(n).wait()
        return carry

    lax.fori_loop(0, 16, drain, 0)

    @pl.when(is_owner)
    def _():
        for n in range(5):
            poly_to_hub(n).wait_send()

    @pl.when(is_hub)
    def _():
        for s in range(3):
            hub_to_twin(s).wait_send()
            hub_to_owner(s).wait_send()
            for n in range(5):
                poly_to_twin(s, n).wait_send()

    sent = x.at[:, pl.ds(0, 16 * (N_ZERO - 1))]
    pltpu.make_async_copy(sent, sent, a_send).wait()
    pltpu.make_async_copy(sent, sent, o_send).wait()
    pltpu.make_async_copy(out_ref, out_ref, o_recv).wait()


def end_kernel(
    lost_ref, back, live, grad, mom, new_ref, update_ref, bv, lv, gv, mv, uv, in_sem, out_sem,
):
    found = lost_ref[0] == 0

    def in_copies(m):
        t, j = m // 3, lax.rem(m, 3)
        return [
            pltpu.make_async_copy(grad.at[m], gv.at[m], in_sem.at[0, m]),
            pltpu.make_async_copy(back.at[t, j], bv.at[t, j], in_sem.at[1, m]),
            pltpu.make_async_copy(back.at[t, 3, :, j], bv.at[t, 3, :, j], in_sem.at[2, m]),
        ]

    def mom_copy(m):
        return pltpu.make_async_copy(mom.at[m], mv.at[m], in_sem.at[3, m])

    def live_copy():
        return pltpu.make_async_copy(live, lv, in_sem.at[4, 0])

    def out_copies(m):
        return [
            pltpu.make_async_copy(mv.at[m], new_ref.at[m], out_sem.at[0, m]),
            pltpu.make_async_copy(uv.at[m], update_ref.at[m], out_sem.at[1, m]),
        ]

    @pl.when(jnp.logical_not(found))
    def _():
        live_copy().start()

    def load(m, carry):
        @pl.when(found)
        def _():
            mom_copy(m).start()

        for copy in in_copies(m):
            copy.start()
        return carry

    lax.fori_loop(0, MATS_GRP, load, 0)

    @pl.when(jnp.logical_not(found))
    def _():
        live_copy().wait()

    def unit(held, m, k):
        t, j = m // 3, lax.rem(m, 3)
        return held[t, j, k // 3, k % 3] if k < 6 else held[t, 3, k - 6, j]

    def matrix(m, carry):
        for copy in in_copies(m):
            copy.wait()

        @pl.when(found)
        def _():
            mom_copy(m).wait()
            mv[m] = gv[m].astype(f32) + beta * mv[m]

        @pl.when(jnp.logical_not(found))
        def _():
            for k in range(CHUNKS):
                span = pl.ds(CHUNK * k, CHUNK)
                held = unit(lv, m, k).astype(f32)
                mv[m, :16, span] = gv[m, :16, span].astype(f32) + beta * held[:, :CHUNK]
                mv[m, 16:, span] = (
                    gv[m, 16:, span].astype(f32) + beta * unpack_rest(held[:, CHUNK:]))

        for k in range(CHUNKS):
            span = pl.ds(CHUNK * k, CHUNK)
            returned = unit(bv, m, k)
            uv[m, :16, span] = returned[:, :CHUNK]
            uv[m, 16:, span] = unpack_rest(returned[:, CHUNK:].astype(f32)).astype(bf16)
        for copy in out_copies(m):
            copy.start()
        return carry

    lax.fori_loop(0, MATS_GRP, matrix, 0)

    def drain(m, carry):
        for copy in out_copies(m):
            copy.wait()
        return carry

    lax.fori_loop(0, MATS_GRP, drain, 0)


def local(grad, momentum, backup, recovery):
    whole = (16, 2, 3, 16, UNIT)
    halves = (16, 3, 16, UNIT)
    shard = (MATS_GRP, ROWS_DEV, MODEL_WIDTH)
    anywhere = pl.BlockSpec(memory_space=pl.ANY)
    scalars = pl.BlockSpec(memory_space=pltpu.SMEM)
    dma = pltpu.SemaphoreType.DMA
    steps = dma((16,))
    returned, live, lost = pl.pallas_call(
        main_kernel,
        out_shape=[jax.ShapeDtypeStruct(whole, bf16)] * 2 + [jax.ShapeDtypeStruct((1,), jnp.int32)],
        in_specs=[scalars] + [anywhere] * 3,
        out_specs=[anywhere] * 2 + [scalars],
        scratch_shapes=[
            pltpu.VMEM(shard, bf16), pltpu.VMEM(shard, f32), pltpu.VMEM(shard, f32),
            pltpu.VMEM(whole, bf16), pltpu.VMEM(halves, bf16), pltpu.VMEM(halves, bf16),
            pltpu.VMEM(whole, bf16), pltpu.VMEM(whole, bf16),
            pltpu.VMEM((3, R, UNIT), bf16), pltpu.VMEM((3, MAIN, UNIT), bf16),
            pltpu.VMEM((MAIN, MAIN), bf16),
            pltpu.VMEM((3, R, R), f32), pltpu.VMEM((3, R, R), bf16), pltpu.VMEM((R, R), f32),
            pltpu.VMEM((3, HALF, R), bf16), pltpu.VMEM((R, R), bf16), pltpu.VMEM((3, R, R), bf16),
            pltpu.VMEM((R, R), bf16), pltpu.VMEM((R, R), bf16),
            pltpu.VMEM((R, R), bf16), pltpu.VMEM((R, R), bf16),
            dma((3, 16)), steps, steps, steps, steps, steps, steps, dma, dma, steps,
            dma((2,)), dma((2,)), dma((3,)), dma((3,)), dma((3,)), dma, dma, dma,
            dma((3, 5)), dma((3, 5)), dma((5,)), dma((3, 5)), dma, dma,
        ],
        compiler_params=pltpu.CompilerParams(
            collective_id=0, has_side_effects=True, vmem_limit_bytes=60 << 20),
    )(recovery, grad, momentum, backup)

    parted = (4, 4, 2, 3, 16, UNIT)
    return pl.pallas_call(
        end_kernel,
        out_shape=[jax.ShapeDtypeStruct(shard, f32), jax.ShapeDtypeStruct(shard, bf16)],
        in_specs=[scalars] + [anywhere] * 4,
        out_specs=[anywhere] * 2,
        scratch_shapes=[
            pltpu.VMEM(parted, bf16), pltpu.VMEM(parted, bf16), pltpu.VMEM(shard, bf16),
            pltpu.VMEM(shard, f32), pltpu.VMEM(shard, bf16),
            dma((5, MATS_GRP)), dma((2, MATS_GRP)),
        ],
        compiler_params=pltpu.CompilerParams(vmem_limit_bytes=60 << 20),
    )(lost, returned.reshape(parted), live.reshape(parted), grad, momentum)


def solution(mesh):
    spread = P("expert", "zero", None)
    return jax.shard_map(
        local, mesh=mesh, in_specs=(spread, spread, spread, P()), out_specs=(spread, spread),
        check_vma=False)
```

```python
import jax
import jax.numpy as jnp
from jax import lax
from jax.experimental import pallas as pl
from jax.experimental.pallas import tpu as pltpu
from jax.sharding import PartitionSpec as P

MODEL_WIDTH = 7168
R = 576
MATS_GRP = 12
ROWS_DEV = 18
N_ZERO = 32
N_EXPERT = 4

beta = 0.95
coef_a = 3.4445
coef_b = -4.775
coef_c = 2.0315
eps = 1e-07
SCALE = 0.2 * max(R, MODEL_WIDTH) ** 0.5

CHUNKS = 8
CHUNK = MODEL_WIDTH // CHUNKS
PIECES = CHUNK // 128
UNIT = CHUNK + 128
MAIN = 16 * N_ZERO
HALF = R // 2

CHIP_OF = (0, 2, 5, 1, 3, 11, 6, 7, 4, 12, 9, 8, 13, 15, 10, 14)
TARGET_OF = tuple(CHIP_OF.index(chip) for chip in range(16))
OWNED = 6 * CHUNK

STEPS = ((0, 0), (1, 0), (0, 1), (3, 0), (0, 3), (2, 0), (0, 2), (1, 1),
         (3, 3), (1, 3), (3, 1), (2, 1), (1, 2), (2, 3), (3, 2), (2, 2))
FAR_FIRST = STEPS[:0:-1] + STEPS[:1]
EVEN_STEPS = tuple(v for v in STEPS if sum(v) % 2 == 0)
ODD_STEPS = tuple(v for v in STEPS if sum(v) % 2 == 1)
HUBS_BEFORE = 6


def order_of(chip):
    x, z = chip // 4, chip % 4
    turns = [TARGET_OF[4 * ((x + dx) % 4) + (z + dz) % 4] for dx, dz in FAR_FIRST]
    for late in range(HUBS_BEFORE, 16):
        if turns[late] % 4 == 3:
            early = max(i for i in range(HUBS_BEFORE) if turns[i] % 4 != 3)
            turns[late], turns[early] = turns[early], turns[late]
    return turns


CODES = tuple(
    tuple(sum(order_of(chip)[4 * part + i] * 16 ** i for i in range(4)) for chip in range(16))
    for part in range(4))

JOIN, LIFT, SEND = 1, 3, 4

MESH = pl.DeviceIdType.MESH
f32 = jnp.float32
bf16 = jnp.bfloat16


def lut(index, table):
    value = jnp.int32(table[0])
    for place, entry in enumerate(table):
        if place:
            value = jnp.where(index == place, jnp.int32(entry), value)
    return value


def pack_rest(rest):
    pieces = [rest[:, 128 * g : 128 * (g + 1)] for g in range(PIECES)]
    return jnp.concatenate(pieces + [jnp.zeros((2, 128), rest.dtype)], axis=0)


def unpack_rest(tile):
    return jnp.concatenate([tile[2 * g : 2 * g + 2] for g in range(PIECES)], axis=1)


def times(left, right):
    return jnp.dot(left, right, preferred_element_type=f32)


def main_kernel(
    recovery, grad, mom, back, out_ref, live_ref, lost_ref,
    gv, mv, bv, own, other, joined, shifted, units, x, o, perm, gram, gsend, gpeer, ghalf, gin, q,
    ma, mb, mc, md,
    in_sem, d_send, d_recv, y_send, y_recv, f_send, f_recv, a_send, a_recv, v_sem,
    g_send, g_recv, h_send, h_recv, k_send, k_recv, i_send, i_recv, q_send, q_recv, p_send, p_recv,
    o_send, o_recv,
):
    zero, expert = lax.axis_index("zero"), lax.axis_index("expert")
    core = lax.rem(zero, 2)
    chip = zero // 2
    cx, cz = chip // 4, lax.rem(chip, 4)
    parity = lax.rem(cx + cz, 2)
    me = lut(chip, TARGET_OF)
    team, spot = me // 4, lax.rem(me, 4)
    is_owner = spot < 3
    is_hub = spot == 3
    twin = zero + 1 - 2 * core
    up = lax.rem(expert + 1, N_EXPERT)
    down = lax.rem(expert + N_EXPERT - 1, N_EXPERT)
    my_rows = pl.ds(16 * (16 * core + 8 * parity + 2 * cx + cz // 2), 16)
    lost = jnp.where(recovery[expert] == zero, 1.0, 0.0)
    mirror = jnp.where(recovery[up] == zero, 1.0, 0.0)
    lost_ref[0] = jnp.where(recovery[expert] == zero, 1, 0)

    barrier = pltpu.get_barrier_semaphore()

    def greet(i, carry):
        pl.semaphore_signal(
            barrier, inc=1, device_id=(lax.rem(zero + i, N_ZERO), expert), device_id_type=MESH)
        return carry

    lax.fori_loop(1, N_ZERO, greet, 0)
    pl.semaphore_signal(barrier, inc=1, device_id=(zero, up), device_id_type=MESH)
    pl.semaphore_signal(barrier, inc=1, device_id=(zero, down), device_id_type=MESH)

    codes = [lut(chip, table) for table in CODES]

    def next_target(i, code):
        fresh = jnp.where(
            i < 4, codes[0], jnp.where(i < 8, codes[1], jnp.where(i < 12, codes[2], codes[3])))
        code = jnp.where(lax.rem(i, 4) == 0, fresh, code // 16)
        return lax.rem(code, 16), code

    def loads(target, source, dest, sem, act):
        t, place = target // 4, lax.rem(target, 4)

        @pl.when(place < 3)
        def _():
            part = (3 * t + place, slice(None), pl.ds(0, OWNED))
            act(pltpu.make_async_copy(source.at[part], dest.at[part], sem))

        @pl.when(place == 3)
        def _():
            part = (pl.ds(3 * t, 3), slice(None), pl.ds(OWNED, MODEL_WIDTH - OWNED))
            act(pltpu.make_async_copy(source.at[part], dest.at[part], sem))

    def back_loads(target, act):
        loads(target, back, bv, in_sem.at[0, target], act)

    def grad_loads(target, act):
        loads(target, grad, gv, in_sem.at[1, target], act)

    def mom_loads(target, act):
        loads(target, mom, mv, in_sem.at[2, target], act)

    def begin(copy):
        copy.start()

    def finish(copy):
        copy.wait()

    def load(i, code):
        target, code = next_target(i, code)
        back_loads(target, begin)
        grad_loads(target, begin)
        mom_loads(target, begin)
        return code

    lax.fori_loop(0, 16, load, jnp.int32(0))

    def sources(target, u):
        t, place = target // 4, lax.rem(target, 4)
        c, s = u // 3, u % 3
        m = 3 * t + jnp.where(place < 3, place, s)
        k = jnp.where(place < 3, 3 * c + s, 6 + c)
        return c, s, m, pl.ds(pl.multiple_of(k * CHUNK, 128), CHUNK)

    def make_own(target):
        back_loads(target, finish)
        for u in range(6):
            c, s, m, span = sources(target, u)
            own[target, c, s, :, :CHUNK] = (bv[m, :16, span] * mirror).astype(bf16)
            own[target, c, s, :, CHUNK:] = pack_rest(bv[m, 16:, span] * mirror).astype(bf16)

    def make_units(target):
        grad_loads(target, finish)
        mom_loads(target, finish)
        stale = (beta * beta) * (1.0 - lost)
        fresh = (beta * beta) * lost
        for u in range(6):
            c, s, m, span = sources(target, u)
            top = (1.0 + beta) * gv[m, :16, span].astype(f32) + stale * mv[m, :16, span]
            units[target, c, s, :, :CHUNK] = (
                top + fresh * shifted[target, c, s, :, :CHUNK].astype(f32)).astype(bf16)
            rest = (1.0 + beta) * gv[m, 16:, span].astype(f32) + stale * mv[m, 16:, span]
            units[target, c, s, :, CHUNK:] = (
                pack_rest(rest) + fresh * shifted[target, c, s, :, CHUNK:].astype(f32)).astype(bf16)

    rows = lax.broadcasted_iota(jnp.int32, (MAIN, MAIN), 0)
    cols = lax.broadcasted_iota(jnp.int32, (MAIN, MAIN), 1)
    wanted = 16 * (lax.rem(rows, 64) // 2) + 2 * (rows // 64) + lax.rem(rows, 2)
    perm[...] = jnp.where(cols == wanted, 1.0, 0.0).astype(bf16)

    first, first_code = next_target(jnp.int32(0), jnp.int32(0))
    make_own(first)

    pl.semaphore_wait(barrier, N_ZERO + 1)

    def to_twin(n):
        return pltpu.make_async_remote_copy(
            own.at[n, 1 - core], other.at[n], d_send.at[n], d_recv.at[n],
            device_id=(twin, expert), device_id_type=MESH)

    def to_up(n):
        return pltpu.make_async_remote_copy(
            joined.at[n], shifted.at[n, core], y_send.at[n], y_recv.at[n],
            device_id=(zero, up), device_id_type=MESH)

    def forward(n):
        return pltpu.make_async_remote_copy(
            shifted.at[n, core], shifted.at[n, core], f_send.at[n], f_recv.at[n],
            device_id=(twin, expert), device_id_type=MESH)

    def keep(n):
        return pltpu.make_async_copy(shifted.at[n], live_ref.at[n], v_sem.at[n])

    def deliver(source, target):
        place = x.at[:, my_rows]

        @pl.when(target != zero)
        def _():
            pltpu.make_async_remote_copy(
                source, place, a_send, a_recv, device_id=(target, expert), device_id_type=MESH).start()

        @pl.when(target == zero)
        def _():
            pltpu.make_async_copy(source, place, a_recv).start()

    def gather_rest():
        pltpu.make_async_copy(x.at[:, pl.ds(0, MAIN)], x.at[:, pl.ds(0, MAIN)], a_recv).wait()
        packed = jnp.concatenate([x[s, :MAIN, CHUNK:] for s in range(3)], axis=1)
        rest = times(perm[...], packed).astype(bf16)
        for s in range(3):
            for g in range(PIECES):
                x[s, MAIN:, 128 * g : 128 * (g + 1)] = (
                    rest[64 * g : 64 * (g + 1), 128 * s : 128 * (s + 1)])

    def gram_of(s, rows=slice(None)):
        return lax.dot_general(
            x[s, rows, :CHUNK], x[s, :, :CHUNK], (((1,), (1,)), ((), ())), preferred_element_type=f32)

    my_half = pl.ds(HALF * core, HALF)
    their_half = pl.ds(HALF - HALF * core, HALF)

    def hub_to_twin(s):
        return pltpu.make_async_remote_copy(
            gsend.at[s, their_half], ghalf.at[s], h_send.at[s], h_recv.at[s],
            device_id=(twin, expert), device_id_type=MESH)

    def hub_to_owner(s):
        return pltpu.make_async_remote_copy(
            ghalf.at[s], gin.at[my_half], k_send.at[s], k_recv,
            device_id=(2 * lut(4 * team + s, CHIP_OF) + core, expert), device_id_type=MESH)

    def pass_on(s):
        hub_to_twin(s).wait_recv()
        ghalf[s] = (gram[s, my_half] + ghalf[s].astype(f32)).astype(bf16)
        hub_to_owner(s).start()

    def stage(i, carry):
        code, past = carry[0], carry[1:]
        now = past[0]

        @pl.when(i < 16)
        def _():
            to_twin(now).start()

        @pl.when(jnp.logical_and(i >= JOIN, i < 16 + JOIN))
        def _():
            to_twin(past[JOIN]).wait_recv()
            joined[past[JOIN]] = own[past[JOIN], core] + other[past[JOIN]]
            to_up(past[JOIN]).start()

        @pl.when(jnp.logical_and(i >= LIFT, i < 16 + LIFT))
        def _():
            to_up(past[LIFT]).wait_recv()
            forward(past[LIFT]).start()

        @pl.when(i >= SEND)
        def _():
            forward(past[SEND]).wait_recv()
            keep(past[SEND]).start()
            make_units(past[SEND])
            for c in range(2):
                deliver(units.at[past[SEND], c], 2 * lut(past[SEND], CHIP_OF) + c)

        later, code = next_target(i + 1, code)

        @pl.when(i + 1 < 16)
        def _():
            make_own(later)

        return (code, later) + past[:SEND]

    lax.fori_loop(0, 16 + SEND, stage, (first_code, first) + (jnp.int32(0),) * SEND)

    def gram_to_twin(n):
        rows = pl.ds(HALF * n, HALF)
        return pltpu.make_async_remote_copy(
            gram.at[0, rows], gpeer.at[rows], g_send.at[n], g_recv.at[n],
            device_id=(twin, expert), device_id_type=MESH)

    def half_to_twin():
        return pltpu.make_async_remote_copy(
            gin.at[my_half], gin.at[my_half], i_send, i_recv,
            device_id=(twin, expert), device_id_type=MESH)

    def part_rows(n):
        return pl.ds(MAIN + 32 * core, 32) if n == 0 else pl.ds(128 * (n - 1) + 64 * core, 64)

    def poly_to_hub(n):
        return pltpu.make_async_remote_copy(
            q.at[0, part_rows(n)], q.at[spot, part_rows(n)], p_send.at[n], p_recv.at[spot, n],
            device_id=(2 * lut(4 * team + 3, CHIP_OF) + core, expert), device_id_type=MESH)

    def poly_to_twin(s, n):
        return pltpu.make_async_remote_copy(
            q.at[s, part_rows(n)], q.at[s, part_rows(n)], q_send.at[s, n], q_recv.at[s, n],
            device_id=(twin, expert), device_id_type=MESH)

    gather_rest()

    @pl.when(is_hub)
    def _():
        for s in range(3):
            part = gram_of(s)
            gram[s] = part
            gsend[s] = part.astype(bf16)
            hub_to_twin(s).start()
            if s:
                pass_on(s - 1)
        pass_on(2)

    @pl.when(is_owner)
    def _():
        for n in range(2):
            rows = slice(HALF * n, HALF * (n + 1))
            gram[0, rows] = gram_of(0, rows) + gram_of(1, rows) + gram_of(2, rows)
            gram_to_twin(n).start()
        pltpu.make_async_copy(gin.at[my_half], gin.at[my_half], k_recv).wait()
        half_to_twin().start()
        gram_to_twin(0).wait()
        gram_to_twin(1).wait()
        total = gram[0] + gpeer[...]
        half_to_twin().wait()
        total = total + gin[...].astype(f32)
        eye = (lax.broadcasted_iota(jnp.int32, (R, R), 0)
               == lax.broadcasted_iota(jnp.int32, (R, R), 1))
        norm = jnp.sqrt(jnp.sum(jnp.where(eye, total, 0.0)))
        inverse = 1.0 / (norm + eps)
        a, b, c = coef_a, coef_b, coef_c
        ga = total * (inverse * inverse)
        ma[...] = ga.astype(bf16)
        gram[0] = ga
        d1 = b * gram[0] + c * times(ma[...], ma[...])
        gram[1] = d1
        mb[...] = d1.astype(bf16)
        mc[...] = (2.0 * a * gram[1] + times(mb[...], mb[...])).astype(bf16)
        a1 = a * a * gram[0] + times(ma[...], mc[...])
        gram[0] = a1
        ma[...] = a1.astype(bf16)
        d2 = b * gram[0] + c * times(ma[...], ma[...])
        gram[2] = d2
        mc[...] = d2.astype(bf16)
        gram[1] = a * (gram[1] + gram[2]) + times(mb[...], mc[...])
        md[...] = (2.0 * a * gram[2] + times(mc[...], mc[...])).astype(bf16)
        a2 = a * a * gram[0] + times(ma[...], md[...])
        gram[0] = a2
        ma[...] = a2.astype(bf16)
        d3 = b * gram[0] + c * times(ma[...], ma[...])
        gram[2] = d3
        mb[...] = d3.astype(bf16)
        mc[...] = gram[1].astype(bf16)
        poly = a * gram[1] + a * a * gram[2] + times(mc[...], mb[...])
        poly = jnp.where(eye, poly + a * a * a, poly)
        q[0] = (poly * (inverse * SCALE)).astype(bf16)
        for n in range(5):
            poly_to_hub(n).start()

    def arrive(n):
        @pl.when(is_hub)
        def _():
            for s in range(3):
                pltpu.make_async_copy(
                    q.at[s, part_rows(n)], q.at[s, part_rows(n)], p_recv.at[s, n]).wait()
                poly_to_twin(s, n).start()
            for s in range(3):
                poly_to_twin(s, n).wait_recv()

    def apply(s, rows):
        which = jnp.where(is_owner, 0, s)
        return times(q[which, rows], x[s, :, :CHUNK]).astype(bf16)

    arrive(0)
    for s in range(3):
        rest = apply(s, pl.ds(MAIN, R - MAIN))
        stacked = jnp.concatenate(
            [rest[:, 128 * g : 128 * (g + 1)] for g in range(PIECES)]
            + [jnp.zeros((64, 128), bf16)], axis=0)
        o[s, :, CHUNK:] = lax.dot_general(
            perm[...], stacked, (((0,), (0,)), ((), ())), preferred_element_type=f32).astype(bf16)

    for n in range(4):
        arrive(n + 1)
        for s in range(3):
            o[s, 128 * n : 128 * (n + 1), :CHUNK] = apply(s, pl.ds(128 * n, 128))
        to_core, to_parity = n // 2, n % 2
        odd = parity != to_parity

        def give(i, carry):
            tx = lax.rem(cx + lut(jnp.where(odd, i + 8, i), [v[0] for v in EVEN_STEPS + ODD_STEPS]), 4)
            tz = lax.rem(cz + lut(jnp.where(odd, i + 8, i), [v[1] for v in EVEN_STEPS + ODD_STEPS]), 4)
            target = 8 * tx + 2 * tz + to_core
            source = o.at[:, pl.ds(128 * n + 16 * (2 * tx + tz // 2), 16)]

            @pl.when(target != zero)
            def _():
                pltpu.make_async_remote_copy(
                    source, out_ref.at[me, core], o_send, o_recv,
                    device_id=(target, expert), device_id_type=MESH).start()

            @pl.when(target == zero)
            def _():
                pltpu.make_async_copy(source, out_ref.at[me, core], o_recv).start()

            return carry

        lax.fori_loop(0, 8, give, 0)

    def drain(n, carry):
        to_twin(n).wait_send()
        to_up(n).wait_send()
        forward(n).wait_send()
        keep(n).wait()
        return carry

    lax.fori_loop(0, 16, drain, 0)

    @pl.when(is_owner)
    def _():
        for n in range(5):
            poly_to_hub(n).wait_send()

    @pl.when(is_hub)
    def _():
        for s in range(3):
            hub_to_twin(s).wait_send()
            hub_to_owner(s).wait_send()
            for n in range(5):
                poly_to_twin(s, n).wait_send()

    sent = x.at[:, pl.ds(0, 16 * (N_ZERO - 1))]
    pltpu.make_async_copy(sent, sent, a_send).wait()
    pltpu.make_async_copy(sent, sent, o_send).wait()
    pltpu.make_async_copy(out_ref, out_ref, o_recv).wait()


def end_kernel(
    lost_ref, back, live, grad, mom, new_ref, update_ref, bv, lv, gv, mv, uv, in_sem, out_sem,
):
    found = lost_ref[0] == 0

    def in_copies(m):
        t, j = m // 3, lax.rem(m, 3)
        return [
            pltpu.make_async_copy(grad.at[m], gv.at[m], in_sem.at[0, m]),
            pltpu.make_async_copy(back.at[t, j], bv.at[t, j], in_sem.at[1, m]),
            pltpu.make_async_copy(back.at[t, 3, :, j], bv.at[t, 3, :, j], in_sem.at[2, m]),
        ]

    def mom_copy(m):
        return pltpu.make_async_copy(mom.at[m], mv.at[m], in_sem.at[3, m])

    def live_copy():
        return pltpu.make_async_copy(live, lv, in_sem.at[4, 0])

    def out_copies(m):
        return [
            pltpu.make_async_copy(mv.at[m], new_ref.at[m], out_sem.at[0, m]),
            pltpu.make_async_copy(uv.at[m], update_ref.at[m], out_sem.at[1, m]),
        ]

    @pl.when(jnp.logical_not(found))
    def _():
        live_copy().start()

    def load(m, carry):
        @pl.when(found)
        def _():
            mom_copy(m).start()

        for copy in in_copies(m):
            copy.start()
        return carry

    lax.fori_loop(0, MATS_GRP, load, 0)

    @pl.when(jnp.logical_not(found))
    def _():
        live_copy().wait()

    def unit(held, m, k):
        t, j = m // 3, lax.rem(m, 3)
        return held[t, j, k // 3, k % 3] if k < 6 else held[t, 3, k - 6, j]

    def matrix(m, carry):
        for copy in in_copies(m):
            copy.wait()

        @pl.when(found)
        def _():
            mom_copy(m).wait()
            mv[m] = gv[m].astype(f32) + beta * mv[m]

        @pl.when(jnp.logical_not(found))
        def _():
            for k in range(CHUNKS):
                span = pl.ds(CHUNK * k, CHUNK)
                held = unit(lv, m, k).astype(f32)
                mv[m, :16, span] = gv[m, :16, span].astype(f32) + beta * held[:, :CHUNK]
                mv[m, 16:, span] = (
                    gv[m, 16:, span].astype(f32) + beta * unpack_rest(held[:, CHUNK:]))

        for k in range(CHUNKS):
            span = pl.ds(CHUNK * k, CHUNK)
            returned = unit(bv, m, k)
            uv[m, :16, span] = returned[:, :CHUNK]
            uv[m, 16:, span] = unpack_rest(returned[:, CHUNK:].astype(f32)).astype(bf16)
        for copy in out_copies(m):
            copy.start()
        return carry

    lax.fori_loop(0, MATS_GRP, matrix, 0)

    def drain(m, carry):
        for copy in out_copies(m):
            copy.wait()
        return carry

    lax.fori_loop(0, MATS_GRP, drain, 0)


def local(grad, momentum, backup, recovery):
    whole = (16, 2, 3, 16, UNIT)
    halves = (16, 3, 16, UNIT)
    shard = (MATS_GRP, ROWS_DEV, MODEL_WIDTH)
    anywhere = pl.BlockSpec(memory_space=pl.ANY)
    scalars = pl.BlockSpec(memory_space=pltpu.SMEM)
    dma = pltpu.SemaphoreType.DMA
    steps = dma((16,))
    returned, live, lost = pl.pallas_call(
        main_kernel,
        out_shape=[jax.ShapeDtypeStruct(whole, bf16)] * 2 + [jax.ShapeDtypeStruct((1,), jnp.int32)],
        in_specs=[scalars] + [anywhere] * 3,
        out_specs=[anywhere] * 2 + [scalars],
        scratch_shapes=[
            pltpu.VMEM(shard, bf16), pltpu.VMEM(shard, f32), pltpu.VMEM(shard, f32),
            pltpu.VMEM(whole, bf16), pltpu.VMEM(halves, bf16), pltpu.VMEM(halves, bf16),
            pltpu.VMEM(whole, bf16), pltpu.VMEM(whole, bf16),
            pltpu.VMEM((3, R, UNIT), bf16), pltpu.VMEM((3, MAIN, UNIT), bf16),
            pltpu.VMEM((MAIN, MAIN), bf16),
            pltpu.VMEM((3, R, R), f32), pltpu.VMEM((3, R, R), bf16), pltpu.VMEM((R, R), f32),
            pltpu.VMEM((3, HALF, R), bf16), pltpu.VMEM((R, R), bf16), pltpu.VMEM((3, R, R), bf16),
            pltpu.VMEM((R, R), bf16), pltpu.VMEM((R, R), bf16),
            pltpu.VMEM((R, R), bf16), pltpu.VMEM((R, R), bf16),
            dma((3, 16)), steps, steps, steps, steps, steps, steps, dma, dma, steps,
            dma((2,)), dma((2,)), dma((3,)), dma((3,)), dma((3,)), dma, dma, dma,
            dma((3, 5)), dma((3, 5)), dma((5,)), dma((3, 5)), dma, dma,
        ],
        compiler_params=pltpu.CompilerParams(
            collective_id=0, has_side_effects=True, vmem_limit_bytes=60 << 20),
    )(recovery, grad, momentum, backup)

    parted = (4, 4, 2, 3, 16, UNIT)
    return pl.pallas_call(
        end_kernel,
        out_shape=[jax.ShapeDtypeStruct(shard, f32), jax.ShapeDtypeStruct(shard, bf16)],
        in_specs=[scalars] + [anywhere] * 4,
        out_specs=[anywhere] * 2,
        scratch_shapes=[
            pltpu.VMEM(parted, bf16), pltpu.VMEM(parted, bf16), pltpu.VMEM(shard, bf16),
            pltpu.VMEM(shard, f32), pltpu.VMEM(shard, bf16),
            dma((5, MATS_GRP)), dma((2, MATS_GRP)),
        ],
        compiler_params=pltpu.CompilerParams(vmem_limit_bytes=60 << 20),
    )(lost, returned.reshape(parted), live.reshape(parted), grad, momentum)


def solution(mesh):
    spread = P("expert", "zero", None)
    return jax.shard_map(
        local, mesh=mesh, in_specs=(spread, spread, spread, P()), out_specs=(spread, spread),
        check_vma=False)
```
